768 devices in a mesh: dp: 64 (over x, y, core), mp: 12 (over z).
Axes of the slice: x: 4, y: 8, z: 12, core: 2. Of those that a mesh axis runs over, the one named last changes fastest.
Arguments:
- features: bfloat16 [30720, 24576], P('dp', 'mp'), may hold values from -6 to 6
- segment: int32 [30720], P(('dp', 'mp')), may hold values from 0 to 1919, never falling along the last dimension, each value on 1 to 48 neighbouring positions
- gains: float32 [3, 8192], replicated, may hold values from 0.25 to 1.75
Outputs:
- mixed: bfloat16 [30720, 8192], P(('dp', 'mp'))
- grad_gains: float32 [3, 8192], replicated
- row_loss: float32 [30720], P(('dp', 'mp'))
The draws below stay inside these ranges and needn't reach their ends.
Inputs may be any that keep to these rules, and one draw needn't show every extreme that they name: `segment`: never falls along the rows; each response spans 1 to 48 rows and one spans exactly 48.
All inputs are finite; a program needn't handle non-finite values.
Results may differ from the reference program's by a relative error of at most 0.001.
Values may be sent and summed in bfloat16 or wider, within the bound.
A program may use at most 64 MiB of HBM per device.

```python
import math
import jax
import jax.numpy as jnp
import numpy as np
from jax import lax

D = 8192
RD = 40
MOST = 48
ROWS = 30720
RESPONSES = 1920
N_MP = 12


def block_scale(key, extent, shards, low, largest):
    def one(position, parts):
        heights = jax.random.uniform(jax.random.fold_in(jax.random.fold_in(key, 6), position), (parts,), jnp.float32, low / len(shards), largest / len(shards))
        return jnp.repeat(jnp.exp(heights), extent[position] // parts).reshape((-1,) + (1,) * (len(extent) - position - 1))

    gain = one(*shards[0])
    for cut in shards[1:]:
        gain = gain * one(*cut)
    return gain


def profile(count, total, most, skew):
    loads = [(1 << 20) // math.isqrt(grade ** skew) + 1 for grade in range(2, count + 1)]
    spare, given = total - most - (count - 1), [1] * (count - 1)
    while spare > 0:
        candidates = [i for i in range(count - 1) if given[i] < most]
        pool, left = sum([loads[i] for i in candidates]), spare
        for i in candidates:
            extra = min(most - given[i], max(1, left * loads[i] // pool), spare)
            given[i] = given[i] + extra
            spare = spare - extra
    return np.array([most] + given)


def uneven(rng, amount, total, bound, skew):
    if amount == 2:
        one = jax.random.randint(rng, (), max(1, total - bound), min(bound, total - 1) + 1)
        return jnp.stack([one, total - one])
    sizes = jnp.asarray(profile(amount, total, bound, skew), jnp.int32)
    pairs = (amount - 1) // 2
    giver, taker = sizes[1:1 + 2 * pairs:2], sizes[2:2 + 2 * pairs:2]
    margin = jnp.minimum(giver - 1, bound - taker)
    shifted = jax.random.randint(jax.random.fold_in(rng, 1), (pairs,), 0, 1 << 20) % (margin + 1)
    sizes = sizes.at[1:1 + 2 * pairs:2].set(giver - shifted).at[2:2 + 2 * pairs:2].set(taker + shifted)
    return sizes[jax.random.permutation(jax.random.fold_in(rng, 2), amount)]


def centred(rng, extent, scale, bound, shards=(), kind=jnp.bfloat16):
    drawn = jax.random.normal(rng, extent, jnp.float32) * scale
    if len(shards) > 0:
        drawn = block_scale(rng, extent, shards, -0.22, 0.18) * drawn
    return jnp.clip(drawn, min=-bound, max=bound).astype(kind)


def setup_inputs(seed: int = 0) -> dict:
    key_list = jax.random.split(jax.random.key(seed), 4)
    return {
        "features": centred(key_list[0], (ROWS, 3 * D), 1.0, 6.0, ((0, 64), (1, 12))),
        "segment": jnp.searchsorted(jnp.cumsum(uneven(key_list[1], RESPONSES, ROWS, MOST, 2)), jnp.arange(ROWS), side="right").astype(jnp.int32),
        "gains": jnp.clip(1.0 + 0.15 * jax.random.normal(key_list[2], (3, D), jnp.float32), 0.25, 1.75),
    }


def block_terms(feat_block, next_block, valid_block, gains):
    x = feat_block.astype(jnp.float32).reshape(feat_block.shape[0], 3, D)
    scale = 1.0 / jnp.sqrt(lax.optimization_barrier(jnp.mean(x * x, axis=2, keepdims=True)) + 1e-06)
    unit = x * scale
    joined = lax.optimization_barrier(jnp.sum(unit * gains[None], axis=1)) / 3.0
    high = next_block.astype(jnp.float32)
    target = high / jnp.sqrt(lax.optimization_barrier(jnp.mean(high * high, axis=1, keepdims=True)) + 1e-06)
    error = joined - target
    size = jnp.abs(error)
    huber = jnp.where(size <= 1.0, 0.5 * error * error, size - 0.5)
    loss = valid_block * lax.optimization_barrier(jnp.mean(huber, axis=1))
    slope = valid_block[:, None] * jnp.clip(error, -1.0, 1.0)
    grad = lax.optimization_barrier(jnp.sum(slope[:, None, :] * unit, axis=0))
    return (joined.astype(jnp.bfloat16), grad, loss)

def reference(features, segment, gains):
    block = RD * N_MP
    count = ROWS // block
    next_high = jnp.concatenate([features[1:, 2 * D:], jnp.zeros((1, D), jnp.bfloat16)], axis=0)
    next_seg = jnp.concatenate([segment[1:], jnp.full((1,), -1, jnp.int32)], axis=0)
    valid = (next_seg == segment).astype(jnp.float32)

    def step(index):
        start = (index * block).astype(jnp.int32)
        feat_block = lax.dynamic_slice_in_dim(features, start, block, 0)
        next_block = lax.dynamic_slice_in_dim(next_high, start, block, 0)
        valid_block = lax.dynamic_slice_in_dim(valid, start, block, 0)
        return block_terms(feat_block, next_block, valid_block, gains)
    mixed_blocks, grads, losses = lax.map(step, jnp.arange(count, dtype=jnp.int32))
    mixed = mixed_blocks.reshape(ROWS, D)
    row_loss = losses.reshape(ROWS)
    grad_gains = lax.optimization_barrier(jnp.sum(grads, axis=0)) / (3.0 * jnp.sqrt(jnp.float32(ROWS)))
    return (mixed, grad_gains, row_loss)
```

```python
import functools
import math

import jax
import jax.numpy as jnp
from jax import lax
from jax.experimental import pallas as pl
from jax.experimental.pallas import tpu as pltpu
from jax.sharding import PartitionSpec as P

LEVELS = 3
QUARTERS = 4
RING = LEVELS * QUARTERS
HALVES = 6
CHUNK = 16
EPS = 1e-06
F32 = jnp.float32
BF16 = jnp.bfloat16


def first_half(level, quarter):
    return (2 * level + (quarter + 1) // 2 - 1 + HALVES) % HALVES


def handler_level(half, quarter):
    return (((half + HALVES + 1 - (quarter + 1) // 2) % HALVES)) // 2


def kernel(sizes, feat, seg, gains, mixed, grads, row_loss, fbuf, xbuf, gbuf, mixbuf, obuf, m1, nr, nrs, nrstage, nrn, nxt,
           sq, segs, scp, cols, val, acc, lq, lrow, lbuf, part, ra, sa, rb, sb, rc, gd,
           local_sem, p1_send, p1_recv, m1_send, m1_recv, mx_send, mx_recv, nr_send, nr_recv, p2_send, p2_recv,
           ls_send, ls_recv, ar_send, ar_recv):
    groups, nx, ny, nk, own, width, total_rows = sizes
    half = 2 * own
    group_rows = HALVES * half
    per_half = half // CHUNK
    chunks = 2 * per_half
    blocks = width // 128
    per_piece = blocks // ny
    lanes = m1.shape[2] - 128

    g, z = lax.axis_index("dp"), lax.axis_index("mp")
    level, quarter = z // QUARTERS, z % QUARTERS
    a = first_half(level, quarter)
    kc = g % nk
    y = (g // nk) % ny
    x = g // (nk * ny)

    def remote(src, dst, send, recv, gd_, zd_):
        return pltpu.make_async_remote_copy(
            src_ref=src, dst_ref=dst, send_sem=send, recv_sem=recv,
            device_id=(gd_, zd_), device_id_type=pl.DeviceIdType.MESH)

    def y_peer(j):
        return (x * ny + (y + j) % ny) * nk + kc

    def xk_peer(j):
        n = (x * nk + kc + j) % (nx * nk)
        return ((n // nk) * ny + y) * nk + n % nk

    loads = []
    for h in range(HALVES):
        loads.append(pltpu.make_async_copy(
            feat.at[pl.ds(h * half, half), :], fbuf.at[pl.ds(h * half, half), :], local_sem.at[h]))
        loads[-1].start()
    gain_load = pltpu.make_async_copy(
        gains.at[:, pl.ds(pl.multiple_of(quarter * width, width), width)], gbuf, local_sem.at[HALVES])
    gain_load.start()
    own_loads = []
    for s in range(2):
        row = pl.multiple_of(((a + s) % HALVES) * half, half)
        own_loads.append(pltpu.make_async_copy(
            feat.at[pl.ds(row, half), :], xbuf.at[level, pl.ds(s * half, half), :], local_sem.at[HALVES + 1 + s]))
        own_loads[-1].start()

    m1[pl.ds(RING, 5), :, 0:lanes] = jnp.zeros((5, 1, lanes), F32)
    m1[pl.ds(RING, 5), :, lanes:lanes + 128] = jnp.full((5, 1, 128), -1.0, F32)
    nr[...] = jnp.zeros(nr.shape, BF16)

    sends_back = jnp.logical_and(jnp.logical_or(z == 0, z >= 2 * QUARTERS), g > 0)
    hears_next = jnp.logical_and(jnp.logical_or(z == 0, z > 2 * QUARTERS), g < groups - 1)
    edge_in = (0, 9, 10, 11)
    edge_out = (8, 9, 10, 11, 0)
    barrier = pltpu.get_barrier_semaphore()

    def greet(gd_, zd_):
        pl.semaphore_signal(barrier, inc=1, device_id=(gd_, zd_), device_id_type=pl.DeviceIdType.MESH)

    for j in range(1, RING):
        greet(g, (z + j) % RING)
    for j in range(1, ny):
        greet(y_peer(j), z)
    for j in range(1, nx * nk):
        greet(xk_peer(j), z)

    @pl.when(sends_back)
    def _():
        for zd in edge_in:
            greet(g - 1, zd)

    @pl.when(hears_next)
    def _():
        for zd in edge_out:
            greet(g + 1, zd)

    sq[pl.ds(group_rows, sq.shape[0] - group_rows), :] = jnp.zeros((sq.shape[0] - group_rows, 128), F32)
    for h in range(HALVES):
        loads[h].wait()

        def squares(i, _):
            row = pl.multiple_of(h * half + i * CHUNK, CHUNK)
            total = jnp.zeros((CHUNK, 128), F32)
            for b in range(blocks):
                v = fbuf[pl.ds(row, CHUNK), 128 * b:128 * b + 128].astype(F32)
                total = total + v * v
            sq[pl.ds(row, CHUNK), :] = total
            return 0

        lax.fori_loop(0, per_half, squares, 0)
    m1[z, :, 0:lanes] = jnp.sum(sq[...].T, axis=0, keepdims=True)
    m1[z, :, lanes:lanes + 128] = seg[...]

    @pl.when(level == LEVELS - 1)
    def _():
        nrs[...] = jnp.zeros(nrs.shape, F32)
        for h in range(HALVES):
            row = ((h + 1) * half) % group_rows
            for b in range(blocks):
                nrs[b:b + 1, :] = fbuf[row:row + CHUNK, 128 * b:128 * b + 128].astype(F32)[0:1, :]
            nrstage[h] = nrs[...].astype(BF16)

    pl.semaphore_wait(
        barrier,
        (RING - 1) + (ny - 1) + (nx * nk - 1) + jnp.where(sends_back, 4, 0) + jnp.where(hears_next, 5, 0))

    def m1_copy(j):
        return remote(m1.at[z], m1.at[z], m1_send.at[j - 1], m1_recv.at[j - 1], g, (z + j) % RING)

    for j in range(1, RING):
        m1_copy(j).start()

    edge_slot = jnp.where(z == 0, 4, quarter)

    def edge_copy(i):
        return remote(m1.at[z], m1.at[RING + edge_slot], mx_send.at[i], mx_recv.at[edge_slot], g - 1, edge_in[i])

    @pl.when(sends_back)
    def _():
        for i in range(4):
            edge_copy(i).start()

    def next_copy(h):
        to = handler_level(h, quarter)
        slot = (h - first_half(to, quarter) + HALVES) % HALVES
        gd_ = g - 1 if h == HALVES - 1 else g
        return remote(nrstage.at[h], nr.at[slot], nr_send.at[h], nr_recv.at[slot], gd_, QUARTERS * to + quarter)

    def next_goes(h):
        if h == HALVES - 1:
            return jnp.logical_and(level == LEVELS - 1, g > 0)
        return jnp.logical_and(level == LEVELS - 1, handler_level(h, quarter) != LEVELS - 1)

    for h in range(HALVES):
        @pl.when(next_goes(h))
        def _():
            next_copy(h).start()

        if h != HALVES - 1:
            @pl.when(jnp.logical_and(level == LEVELS - 1, handler_level(h, quarter) == LEVELS - 1))
            def _():
                slot = (h - first_half(LEVELS - 1, quarter) + HALVES) % HALVES
                nr[slot] = nrstage[h]

    def level_copy(d, k):
        to = (level + d) % LEVELS
        s, kk = k // per_half, k % per_half
        row = ((first_half(to, quarter) + s) % HALVES) * half + kk * CHUNK
        return remote(
            feat.at[pl.ds(pl.multiple_of(row, CHUNK), CHUNK), :],
            xbuf.at[level, pl.ds(pl.multiple_of(k * CHUNK, CHUNK), CHUNK), :],
            p1_send.at[d - 1, k], p1_recv.at[d - 1, k], g, QUARTERS * to + quarter)

    def level_start(i, _):
        k = chunks - 1 - i
        level_copy(1, k).start()
        level_copy(2, k).start()
        return 0

    lax.fori_loop(0, chunks, level_start, 0)

    acc[...] = jnp.zeros(acc.shape, F32)
    lq[...] = jnp.zeros(lq.shape, F32)
    scp[...] = jnp.zeros(scp.shape, F32)
    segs[...] = jnp.zeros(segs.shape, F32)
    gain_load.wait()
    gbuf[...] = gbuf[...] * (1.0 / LEVELS)

    for j in range(1, RING):
        m1_copy(j).wait_recv()

    @pl.when(hears_next)
    def _():
        for i in range(5):
            remote(m1.at[z], m1.at[RING + i], mx_send.at[0], mx_recv.at[i], g, (z + 1) % RING).wait_recv()

    def scale_of(first):
        total = m1[first, :, 0:lanes]
        for i in range(1, QUARTERS):
            total = total + m1[first + i, :, 0:lanes]
        return 1.0 / jnp.sqrt(total * (1.0 / (QUARTERS * width)) + EPS)

    for l in range(LEVELS):
        scp[l:l + 1, :] = scale_of(QUARTERS * l)
    for o in range(RING):
        segs[o:o + 1, :] = m1[o, :, lanes:lanes + 128]
    segs[RING:RING + 1, :] = m1[RING + 4, :, lanes:lanes + 128]
    here = segs[...]
    lane = lax.broadcasted_iota(jnp.int32, here.shape, 1)
    after = jnp.where(lane == own - 1, pltpu.roll(pltpu.roll(here, 15, 0), own - 1, 1), pltpu.roll(here, 127, 1))
    scp[16:32, 0:128] = jnp.where(after == here, 1.0, 0.0)
    cols[...] = scp[...].T
    for o in range(RING):
        val[own * o:own * o + own, :] = jnp.broadcast_to(cols[0:own, 16 + o:17 + o], (own, 128))
    cols[group_rows:group_rows + 8, :] = jnp.broadcast_to(scale_of(RING)[:, 0:1], (8, 128))

    for s in range(2):
        h = (a + s) % HALVES
        comes = jnp.logical_or(jnp.logical_and(h == HALVES - 1, g < groups - 1),
                               jnp.logical_and(h != HALVES - 1, level != LEVELS - 1))

        @pl.when(comes)
        def _():
            remote(nrstage.at[0], nr.at[s], nr_send.at[0], nr_recv.at[s], g, (z + 1) % RING).wait_recv()

        factor = cols[pl.ds(pl.multiple_of((h + 1) * half, 8), 8), :][0:1, LEVELS - 1:LEVELS]
        nrn[s] = nr[s].astype(F32) * factor
    for s in range(2):
        own_loads[s].wait()

    last = lax.broadcasted_iota(jnp.int32, (CHUNK, 128), 0) == CHUNK - 1

    def work(i, _):
        k = chunks - 1 - i
        s, kk = k // per_half, k % per_half
        row = pl.multiple_of(((a + s) % HALVES) * half + kk * CHUNK, CHUNK)
        at = pl.multiple_of(k * CHUNK, CHUNK)
        level_copy(1, k).wait_recv()
        level_copy(2, k).wait_recv()

        @pl.when(kk == per_half - 1)
        def _():
            nxt[...] = nrn[s]

        tile = cols[pl.ds(row, CHUNK), :]
        scales = [jnp.broadcast_to(tile[:, l:l + 1], (CHUNK, 128)) for l in range(LEVELS)]
        ok = val[pl.ds(row, CHUNK), :]
        loss = jnp.zeros((CHUNK, 128), F32)
        for b in range(blocks):
            cs = slice(128 * b, 128 * b + 128)
            unit = [xbuf[l, pl.ds(at, CHUNK), cs].astype(F32) * scales[l] for l in range(LEVELS)]
            joined = unit[0] * gbuf[0:1, cs] + unit[1] * gbuf[1:2, cs] + unit[2] * gbuf[2:3, cs]
            mixbuf[pl.ds(at, CHUNK), cs] = joined.astype(BF16)
            target = jnp.where(last, nxt[b:b + 1, :], pltpu.roll(unit[2], CHUNK - 1, 0))
            nxt[b:b + 1, :] = unit[2][0:1, :]
            error = joined - target
            slope = jnp.clip(error, -1.0, 1.0)
            loss = loss + slope * (error - 0.5 * slope)
            slope = slope * ok
            for l in range(LEVELS):
                term = slope * unit[l]
                acc[l, :, cs] = acc[l, :, cs] + (term[0:8] + term[8:16])
        lq[s, pl.ds(pl.multiple_of(kk * CHUNK, CHUNK), CHUNK), :] = loss * ok
        return 0

    lax.fori_loop(0, chunks, work, 0)

    factor = 1.0 / (math.sqrt(total_rows) * LEVELS)
    part[...] = jnp.zeros(part.shape, F32)
    for l in range(LEVELS):
        for b in range(blocks):
            r = l * per_piece + b % per_piece
            part[b // per_piece, r:r + 1, :] = factor * jnp.sum(acc[l, :, 128 * b:128 * b + 128], axis=0, keepdims=True)

    def a_copy(j):
        return remote(part.at[(y + j) % ny], ra.at[y], ar_send.at[0, j], ar_recv.at[0, j], y_peer(j), z)

    for j in range(1, ny):
        a_copy(j).start()
    ra[y] = part[y]

    for s in range(2):
        lrow[s] = jnp.sum(lq[s].T, axis=0, keepdims=True)

    def mixed_copy(s, q):
        owner = 2 * ((a + s) % HALVES) + q
        return owner, remote(mixbuf.at[pl.ds(s * half + 32 * q, 48), :], obuf.at[quarter],
                             p2_send.at[2 * s + q], p2_recv.at[quarter], g, owner)

    def loss_copy(s, q):
        owner = 2 * ((a + s) % HALVES) + q
        return owner, remote(lrow.at[s], lbuf.at[quarter], ls_send.at[2 * s + q], ls_recv.at[quarter], g, owner)

    for s in range(2):
        for q in range(2):
            owner, copy = mixed_copy(s, q)
            _, small = loss_copy(s, q)

            @pl.when(owner != z)
            def _():
                copy.start()
                small.start()

            @pl.when(owner == z)
            def _():
                obuf[quarter] = mixbuf[s * half + 32 * q:s * half + 32 * q + 48, :]
                lbuf[quarter] = lrow[s]

    for j in range(1, ny):
        a_copy(j).wait_recv()
    total = ra[0]
    for j in range(1, ny):
        total = total + ra[j]
    sa[...] = total

    me = x * nk + kc

    def b_copy(j):
        return remote(sa, rb.at[me], ar_send.at[1, j], ar_recv.at[1, j], xk_peer(j), z)

    for j in range(1, nx * nk):
        b_copy(j).start()
    rb[me] = sa[...]
    for j in range(1, nx * nk):
        b_copy(j).wait_recv()
    total = rb[0]
    for j in range(1, nx * nk):
        total = total + rb[j]
    sb[...] = total

    def c_copy(j):
        return remote(sb, rc.at[level], ar_send.at[2, j], ar_recv.at[2, j], g, (z + QUARTERS * j) % RING)

    for j in range(1, LEVELS):
        c_copy(j).start()
    rc[level] = sb[...]
    for j in range(1, LEVELS):
        c_copy(j).wait_recv()
    gd[y, quarter] = rc[0] + rc[1] + rc[2]

    def d_copy(j):
        return remote(gd.at[y, quarter], gd.at[y, quarter], ar_send.at[3, j], ar_recv.at[3, j],
                      g, QUARTERS * level + (quarter + j) % QUARTERS)

    for j in range(1, QUARTERS):
        d_copy(j).start()
    for j in range(1, QUARTERS):
        d_copy(j).wait_recv()

    def e_copy(j):
        return remote(gd.at[y], gd.at[y], ar_send.at[4, j], ar_recv.at[4, j], y_peer(j), z)

    for j in range(1, ny):
        e_copy(j).start()

    mine, odd = z // 2, z % 2
    for i in range(QUARTERS):
        @pl.when(QUARTERS * handler_level(mine, i) + i != z)
        def _():
            remote(mixbuf.at[pl.ds(0, 48), :], obuf.at[i], p2_send.at[0], p2_recv.at[i], g, (z + 1) % RING).wait_recv()
            remote(lrow.at[0], lbuf.at[i], ls_send.at[0], ls_recv.at[i], g, (z + 1) % RING).wait_recv()

    total = lbuf[0] + lbuf[1] + lbuf[2] + lbuf[3]
    row_loss[...] = total * (1.0 / (QUARTERS * width))

    @pl.when(odd == 0)
    def _():
        for i in range(QUARTERS):
            mixed[:, i * width:(i + 1) * width] = obuf[i, 0:own, :]

    @pl.when(odd == 1)
    def _():
        for i in range(QUARTERS):
            for b in range(0, width, 256):
                rows = obuf[i, :, b:b + 256].astype(F32)
                mixed[:, i * width + b:i * width + b + 256] = rows[8:8 + own, :].astype(BF16)

    for j in range(1, ny):
        e_copy(j).wait_recv()
    for q in range(QUARTERS):
        for j in range(ny):
            for l in range(LEVELS):
                for i in range(per_piece):
                    at = q * width + (j * per_piece + i) * 128
                    grads[l:l + 1, at:at + 128] = gd[j, q, l * per_piece + i:l * per_piece + i + 1, :]

    for j in range(1, RING):
        m1_copy(j).wait_send()

    @pl.when(sends_back)
    def _():
        for i in range(4):
            edge_copy(i).wait_send()

    for h in range(HALVES):
        @pl.when(next_goes(h))
        def _():
            next_copy(h).wait_send()

    def level_sent(k, _):
        level_copy(1, k).wait_send()
        level_copy(2, k).wait_send()
        return 0

    lax.fori_loop(0, chunks, level_sent, 0)
    for s in range(2):
        for q in range(2):
            owner, copy = mixed_copy(s, q)
            _, small = loss_copy(s, q)

            @pl.when(owner != z)
            def _():
                copy.wait_send()
                small.wait_send()

    for j in range(1, ny):
        a_copy(j).wait_send()
        e_copy(j).wait_send()
    for j in range(1, nx * nk):
        b_copy(j).wait_send()
    for j in range(1, LEVELS):
        c_copy(j).wait_send()
    for j in range(1, QUARTERS):
        d_copy(j).wait_send()


def solution(mesh):
    groups = mesh.shape["dp"]
    nk = 2
    ny = 8 if groups == 64 else groups // nk
    nx = groups // (nk * ny)

    def shards(features, segment, gains):
        rows, width = features.shape
        own = rows // RING
        sizes = (groups, nx, ny, nk, own, width, rows * groups)
        half = 2 * own
        lanes = -(-rows // 128) * 128
        seg = jnp.pad(segment.astype(F32).reshape(1, own), ((0, 0), (0, 128 - own)))
        vmem = pl.BlockSpec(memory_space=pltpu.VMEM)
        hbm = pl.BlockSpec(memory_space=pl.ANY)
        dma = pltpu.SemaphoreType.DMA
        chunks = 2 * half // CHUNK
        mixed, grads, row_loss = pl.pallas_call(
            functools.partial(kernel, sizes),
            out_shape=(
                jax.ShapeDtypeStruct((own, QUARTERS * width), BF16),
                jax.ShapeDtypeStruct((LEVELS, QUARTERS * width), F32),
                jax.ShapeDtypeStruct((1, 128), F32),
            ),
            in_specs=[hbm, vmem, hbm],
            out_specs=(vmem, vmem, vmem),
            scratch_shapes=[
                pltpu.VMEM((rows, width), BF16),
                pltpu.VMEM((LEVELS, 2 * half, width), BF16),
                pltpu.VMEM((LEVELS, width), F32),
                pltpu.VMEM((2 * half, width), BF16),
                pltpu.VMEM((QUARTERS, 48, width), BF16),
                pltpu.VMEM((RING + 5, 1, lanes + 128), F32),
                pltpu.VMEM((2, 16, 128), BF16),
                pltpu.VMEM((16, 128), F32),
                pltpu.VMEM((HALVES, 16, 128), BF16),
                pltpu.VMEM((2, 16, 128), F32),
                pltpu.VMEM((16, 128), F32),
                pltpu.VMEM((lanes, 128), F32),
                pltpu.VMEM((16, 128), F32),
                pltpu.VMEM((128, lanes), F32),
                pltpu.VMEM((lanes, 128), F32),
                pltpu.VMEM((rows, 128), F32),
                pltpu.VMEM((LEVELS, 8, width), F32),
                pltpu.VMEM((2, 128, 128), F32),
                pltpu.VMEM((2, 1, 128), F32),
                pltpu.VMEM((QUARTERS, 1, 128), F32),
                pltpu.VMEM((ny, 8, 128), F32),
                pltpu.VMEM((ny, 8, 128), F32),
                pltpu.VMEM((8, 128), F32),
                pltpu.VMEM((nx * nk, 8, 128), F32),
                pltpu.VMEM((8, 128), F32),
                pltpu.VMEM((LEVELS, 8, 128), F32),
                pltpu.VMEM((ny, QUARTERS, 8, 128), F32),
                dma((HALVES + 3,)),
                dma((2, chunks)), dma((2, chunks)),
                dma((RING - 1,)), dma((RING - 1,)),
                dma((4,)), dma((5,)),
                dma((HALVES,)), dma((2,)),
                dma((4,)), dma((QUARTERS,)),
                dma((4,)), dma((QUARTERS,)),
                dma((5, 8)), dma((5, 8)),
            ],
            compiler_params=pltpu.CompilerParams(
                collective_id=0, has_side_effects=True, vmem_limit_bytes=32 * 1024 * 1024),
        )(features, seg, gains)
        start = (lax.axis_index("mp") % 2) * own
        row_loss = lax.dynamic_slice_in_dim(row_loss.reshape(128), start, own, 0)
        return mixed, grads, row_loss

    return jax.shard_map(
        shards,
        mesh=mesh,
        in_specs=(P("dp", "mp"), P(("dp", "mp")), P()),
        out_specs=(P(("dp", "mp"), None), P(), P(("dp", "mp"))),
        check_vma=False,
    )
```

```python
import functools
import math

import jax
import jax.numpy as jnp
from jax import lax
from jax.experimental import pallas as pl
from jax.experimental.pallas import tpu as pltpu
from jax.sharding import PartitionSpec as P

LEVELS = 3
QUARTERS = 4
RING = LEVELS * QUARTERS
HALVES = 6
CHUNK = 16
EPS = 1e-06
F32 = jnp.float32
BF16 = jnp.bfloat16


def first_half(level, quarter):
    return (2 * level + (quarter + 1) // 2 - 1 + HALVES) % HALVES


def handler_level(half, quarter):
    return (((half + HALVES + 1 - (quarter + 1) // 2) % HALVES)) // 2


def kernel(sizes, feat, seg, gains, mixed, grads, row_loss, fbuf, xbuf, gbuf, segbuf, mixbuf, obuf, m1, nr, nrs, nrstage, nrn, nxt,
           sq, segs, scp, cols, val, acc, lq, lrow, lbuf, part, kb, sa, rb, rc, gf,
           local_sem, p1_send, p1_recv, m1_send, m1_recv, mx_send, mx_recv, nr_send, nr_recv, p2_send, p2_recv,
           ls_send, ls_recv, k_sem, xy_sem, z_sem, y_send, y_recv, f_send, f_recv):
    groups, nx, ny, nk, own, width, total_rows = sizes
    half = 2 * own
    group_rows = HALVES * half
    per_half = half // CHUNK
    chunks = 2 * per_half
    blocks = width // 128
    per_piece = blocks // (ny * nk)
    lanes = m1.shape[2] - 128

    g, z = lax.axis_index("dp"), lax.axis_index("mp")
    level, quarter = lax.div(z, QUARTERS), lax.rem(z, QUARTERS)
    a = first_half(level, quarter)
    kc = lax.rem(g, nk)
    y = lax.rem(lax.div(g, nk), ny)
    x = lax.div(g, nk * ny)
    xs = [lax.rem(x + i, nx) * (ny * nk) + kc for i in range(nx)]
    ys = [lax.rem(y + i, ny) for i in range(ny)]
    zs = [lax.rem(z + i, RING) for i in range(RING)]
    plane = [(dx, dy) for dx in range(nx) for dy in range(ny)][1:]
    other = g + 1 - 2 * kc

    def remote(src, dst, send, recv, gd_, zd_):
        return pltpu.make_async_remote_copy(
            src_ref=src, dst_ref=dst, send_sem=send, recv_sem=recv,
            device_id=(gd_, zd_), device_id_type=pl.DeviceIdType.MESH)

    loads = []
    for h in range(HALVES):
        loads.append(pltpu.make_async_copy(
            feat.at[pl.ds(h * half, half), :], fbuf.at[pl.ds(h * half, half), :], local_sem.at[h]))
        loads[-1].start()
    gain_load = pltpu.make_async_copy(
        gains.at[:, pl.ds(pl.multiple_of(quarter * width, width), width)], gbuf, local_sem.at[HALVES])
    gain_load.start()
    seg_load = pltpu.make_async_copy(seg, segbuf, local_sem.at[HALVES + 3])
    seg_load.start()
    own_loads = []
    for s in range(2):
        row = pl.multiple_of(((a + s) % HALVES) * half, half)
        own_loads.append(pltpu.make_async_copy(
            feat.at[pl.ds(row, half), :], xbuf.at[level, pl.ds(s * half, half), :], local_sem.at[HALVES + 1 + s]))
        own_loads[-1].start()

    m1[pl.ds(RING, 5), :, 0:lanes] = jnp.zeros((5, 1, lanes), F32)
    m1[pl.ds(RING, 5), :, lanes:lanes + 128] = jnp.full((5, 1, 128), -1.0, F32)
    nr[...] = jnp.zeros(nr.shape, BF16)

    sends_back = jnp.logical_and(jnp.logical_or(z == 0, z >= 2 * QUARTERS), g > 0)
    hears_next = jnp.logical_and(jnp.logical_or(z == 0, z > 2 * QUARTERS), g < groups - 1)
    edge_in = (0, 9, 10, 11)
    edge_out = (8, 9, 10, 11, 0)
    barrier = pltpu.get_barrier_semaphore()

    def greet(gd_, zd_):
        pl.semaphore_signal(barrier, inc=1, device_id=(gd_, zd_), device_id_type=pl.DeviceIdType.MESH)

    for j in (QUARTERS, 2 * QUARTERS, 1, 11, 2, 10, 3, 9, 5, 7, 6):
        greet(g, zs[j])
    greet(other, z)
    for dx, dy in plane:
        greet(xs[dx] + ys[dy] * nk, z)

    @pl.when(sends_back)
    def _():
        for zd in edge_in:
            greet(g - 1, zd)

    @pl.when(hears_next)
    def _():
        for zd in edge_out:
            greet(g + 1, zd)

    sq[pl.ds(group_rows, sq.shape[0] - group_rows), :] = jnp.zeros((sq.shape[0] - group_rows, 128), F32)
    for h in range(HALVES):
        loads[h].wait()

        def squares(i, _):
            row = pl.multiple_of(h * half + i * CHUNK, CHUNK)
            total = jnp.zeros((CHUNK, 128), F32)
            for b in range(blocks):
                v = fbuf[pl.ds(row, CHUNK), 128 * b:128 * b + 128].astype(F32)
                total = total + v * v
            sq[pl.ds(row, CHUNK), :] = total
            return 0

        lax.fori_loop(0, per_half, squares, 0)
    m1[z, :, 0:lanes] = jnp.sum(sq[...].T, axis=0, keepdims=True)
    seg_load.wait()
    m1[z, :, lanes:lanes + 128] = jnp.zeros((1, 128), F32)
    m1[z, :, lanes:lanes + own] = segbuf[...].astype(F32)

    @pl.when(level == LEVELS - 1)
    def _():
        nrs[...] = jnp.zeros(nrs.shape, F32)
        for h in range(HALVES):
            row = ((h + 1) * half) % group_rows
            for b in range(blocks):
                nrs[b:b + 1, :] = fbuf[row:row + CHUNK, 128 * b:128 * b + 128].astype(F32)[0:1, :]
            nrstage[h] = nrs[...].astype(BF16)

    pl.semaphore_wait(
        barrier, RING - 1 + nk - 1 + len(plane) + jnp.where(sends_back, 4, 0) + jnp.where(hears_next, 5, 0))

    def m1_copy(j):
        return remote(m1.at[z], m1.at[z], m1_send.at[j - 1], m1_recv.at[j - 1], g, zs[j])

    for j in range(1, RING):
        m1_copy(j).start()

    edge_slot = jnp.where(z == 0, 4, quarter)

    def edge_copy(i):
        return remote(m1.at[z], m1.at[RING + edge_slot], mx_send.at[i], mx_recv.at[edge_slot], g - 1, edge_in[i])

    @pl.when(sends_back)
    def _():
        for i in range(4):
            edge_copy(i).start()

    def next_copy(h):
        to = handler_level(h, quarter)
        slot = (h - first_half(to, quarter) + HALVES) % HALVES
        gd_ = g - 1 if h == HALVES - 1 else g
        return remote(nrstage.at[h], nr.at[slot], nr_send.at[h], nr_recv.at[slot], gd_, QUARTERS * to + quarter)

    def next_goes(h):
        if h == HALVES - 1:
            return jnp.logical_and(level == LEVELS - 1, g > 0)
        return jnp.logical_and(level == LEVELS - 1, handler_level(h, quarter) != LEVELS - 1)

    for h in range(HALVES):
        @pl.when(next_goes(h))
        def _():
            next_copy(h).start()

        if h != HALVES - 1:
            @pl.when(jnp.logical_and(level == LEVELS - 1, handler_level(h, quarter) == LEVELS - 1))
            def _():
                slot = (h - first_half(LEVELS - 1, quarter) + HALVES) % HALVES
                nr[slot] = nrstage[h]

    def level_copy(d, k):
        to = (level + d) % LEVELS
        s, kk = k // per_half, k % per_half
        row = ((first_half(to, quarter) + s) % HALVES) * half + kk * CHUNK
        return remote(
            feat.at[pl.ds(pl.multiple_of(row, CHUNK), CHUNK), :],
            xbuf.at[level, pl.ds(pl.multiple_of(k * CHUNK, CHUNK), CHUNK), :],
            p1_send.at[d - 1, k], p1_recv.at[d - 1, k], g, QUARTERS * to + quarter)

    def level_start(i, _):
        k = chunks - 1 - i
        level_copy(1, k).start()
        level_copy(2, k).start()
        return 0

    lax.fori_loop(0, chunks, level_start, 0)

    acc[...] = jnp.zeros(acc.shape, F32)
    lq[...] = jnp.zeros(lq.shape, F32)
    scp[...] = jnp.zeros(scp.shape, F32)
    segs[...] = jnp.zeros(segs.shape, F32)
    gain_load.wait()
    gbuf[...] = gbuf[...] * (1.0 / LEVELS)

    for j in range(1, RING):
        m1_copy(j).wait_recv()

    @pl.when(hears_next)
    def _():
        for i in range(5):
            remote(m1.at[z], m1.at[RING + i], mx_send.at[0], mx_recv.at[i], g, (z + 1) % RING).wait_recv()

    def scale_of(first):
        total = m1[first, :, 0:lanes]
        for i in range(1, QUARTERS):
            total = total + m1[first + i, :, 0:lanes]
        return 1.0 / jnp.sqrt(total * (1.0 / (QUARTERS * width)) + EPS)

    for l in range(LEVELS):
        scp[l:l + 1, :] = scale_of(QUARTERS * l)
    for o in range(RING):
        segs[o:o + 1, :] = m1[o, :, lanes:lanes + 128]
    segs[RING:RING + 1, :] = m1[RING + 4, :, lanes:lanes + 128]
    here = segs[...]
    lane = lax.broadcasted_iota(jnp.int32, here.shape, 1)
    after = jnp.where(lane == own - 1, pltpu.roll(pltpu.roll(here, 15, 0), own - 1, 1), pltpu.roll(here, 127, 1))
    scp[16:32, 0:128] = jnp.where(after == here, 1.0, 0.0)
    cols[...] = scp[...].T
    for o in range(RING):
        val[own * o:own * o + own, :] = jnp.broadcast_to(cols[0:own, 16 + o:17 + o], (own, 128))
    cols[group_rows:group_rows + 8, :] = jnp.broadcast_to(scale_of(RING)[:, 0:1], (8, 128))

    for s in range(2):
        h = (a + s) % HALVES
        comes = jnp.logical_or(jnp.logical_and(h == HALVES - 1, g < groups - 1),
                               jnp.logical_and(h != HALVES - 1, level != LEVELS - 1))

        @pl.when(comes)
        def _():
            remote(nrstage.at[0], nr.at[s], nr_send.at[0], nr_recv.at[s], g, (z + 1) % RING).wait_recv()

        factor = cols[pl.ds(pl.multiple_of((h + 1) * half, 8), 8), :][0:1, LEVELS - 1:LEVELS]
        nrn[s] = nr[s].astype(F32) * factor
    for s in range(2):
        own_loads[s].wait()

    last = lax.broadcasted_iota(jnp.int32, (CHUNK, 128), 0) == CHUNK - 1

    def work(i, _):
        k = chunks - 1 - i
        s, kk = k // per_half, k % per_half
        row = pl.multiple_of(((a + s) % HALVES) * half + kk * CHUNK, CHUNK)
        at = pl.multiple_of(k * CHUNK, CHUNK)
        level_copy(1, k).wait_recv()
        level_copy(2, k).wait_recv()

        @pl.when(kk == per_half - 1)
        def _():
            nxt[...] = nrn[s]

        tile = cols[pl.ds(row, CHUNK), :]
        scales = [jnp.broadcast_to(tile[:, l:l + 1], (CHUNK, 128)) for l in range(LEVELS)]
        ok = val[pl.ds(row, CHUNK), :]
        loss = jnp.zeros((CHUNK, 128), F32)
        for b in range(blocks):
            cs = slice(128 * b, 128 * b + 128)
            unit = [xbuf[l, pl.ds(at, CHUNK), cs].astype(F32) * scales[l] for l in range(LEVELS)]
            joined = unit[0] * gbuf[0:1, cs] + unit[1] * gbuf[1:2, cs] + unit[2] * gbuf[2:3, cs]
            mixbuf[pl.ds(at, CHUNK), cs] = joined.astype(BF16)
            target = jnp.where(last, nxt[b:b + 1, :], pltpu.roll(unit[2], CHUNK - 1, 0))
            nxt[b:b + 1, :] = unit[2][0:1, :]
            error = joined - target
            slope = jnp.clip(error, -1.0, 1.0)
            loss = loss + slope * (error - 0.5 * slope)
            slope = slope * ok
            for l in range(LEVELS):
                term = slope * unit[l]
                acc[l, :, cs] = acc[l, :, cs] + (term[0:8] + term[8:16])
        lq[s, pl.ds(pl.multiple_of(kk * CHUNK, CHUNK), CHUNK), :] = loss * ok
        return 0

    lax.fori_loop(0, chunks, work, 0)

    factor = 1.0 / (math.sqrt(total_rows) * LEVELS)
    part[...] = jnp.zeros(part.shape, F32)
    for b in range(blocks):
        for l in range(LEVELS):
            part[b % nk, b // nk, l:l + 1, :] = factor * jnp.sum(acc[l, :, 128 * b:128 * b + 128], axis=0, keepdims=True)
    k_copy = remote(part.at[1 - kc], kb, k_sem.at[0], k_sem.at[1], other, z)
    k_copy.start()

    for s in range(2):
        lrow[s] = jnp.sum(lq[s].T, axis=0, keepdims=True)

    k_copy.wait_recv()
    sa[...] = part[kc] + kb[...]

    def xy_copy(n):
        dx, dy = plane[n]
        return remote(sa.at[ys[dy]], rb.at[n], xy_sem.at[0], xy_sem.at[1], xs[dx] + ys[dy] * nk, z)

    for n in range(len(plane)):
        xy_copy(n).start()

    def mixed_copy(s, q):
        owner = 2 * ((a + s) % HALVES) + q
        return owner, remote(mixbuf.at[pl.ds(s * half + 32 * q, 48), :], obuf.at[quarter],
                             p2_send.at[2 * s + q], p2_recv.at[quarter], g, owner)

    def loss_copy(s, q):
        owner = 2 * ((a + s) % HALVES) + q
        return owner, remote(lrow.at[s], lbuf.at[quarter], ls_send.at[2 * s + q], ls_recv.at[quarter], g, owner)

    for s in range(2):
        for q in range(2):
            owner, copy = mixed_copy(s, q)
            _, small = loss_copy(s, q)

            @pl.when(owner != z)
            def _():
                copy.start()
                small.start()

            @pl.when(owner == z)
            def _():
                obuf[quarter] = mixbuf[s * half + 32 * q:s * half + 32 * q + 48, :]
                lbuf[quarter] = lrow[s]

    for j in range(1, RING):
        m1_copy(j).wait_send()

    @pl.when(sends_back)
    def _():
        for i in range(4):
            edge_copy(i).wait_send()

    for h in range(HALVES):
        @pl.when(next_goes(h))
        def _():
            next_copy(h).wait_send()

    def level_sent(k, _):
        level_copy(1, k).wait_send()
        level_copy(2, k).wait_send()
        return 0

    lax.fori_loop(0, chunks, level_sent, 0)
    pltpu.make_async_copy(rb, rb, xy_sem.at[1]).wait()
    total = sa[y]
    for n in range(len(plane)):
        total = total + rb[n]
    rc[0] = total

    def z_copy(j):
        return remote(rc.at[0], rc.at[j], z_sem.at[0], z_sem.at[1], g, zs[j])

    for j in range(1, RING):
        z_copy(j).start()
    landed = rc.at[pl.ds(1, RING - 1)]
    pltpu.make_async_copy(landed, landed, z_sem.at[1]).wait()
    for j in range(QUARTERS):
        gf[kc, y, lax.rem(quarter + QUARTERS - j, QUARTERS)] = rc[j] + rc[j + QUARTERS] + rc[j + 2 * QUARTERS]

    def y_copy(j):
        return remote(gf.at[kc, y], gf.at[kc, y], y_send.at[j], y_recv.at[j], xs[0] + ys[j] * nk, z)

    def f_copy(j):
        at = lax.rem(y + ny - j, ny)
        return remote(gf.at[kc, at], gf.at[kc, at], f_send.at[j], f_recv.at[j], other, z)

    for j in range(1, ny):
        y_copy(j).start()
    f_copy(0).start()

    mine, odd = z // 2, z % 2
    for i in range(QUARTERS):
        @pl.when(QUARTERS * handler_level(mine, i) + i != z)
        def _():
            remote(mixbuf.at[pl.ds(0, 48), :], obuf.at[i], p2_send.at[0], p2_recv.at[i], g, (z + 1) % RING).wait_recv()
            remote(lrow.at[0], lbuf.at[i], ls_send.at[0], ls_recv.at[i], g, (z + 1) % RING).wait_recv()

    total = lbuf[0] + lbuf[1] + lbuf[2] + lbuf[3]
    total = total * (1.0 / (QUARTERS * width))
    row_loss[...] = jnp.where(odd == 0, total[:, 0:own], total[:, own:2 * own])

    @pl.when(odd == 0)
    def _():
        for i in range(QUARTERS):
            mixed[:, i * width:(i + 1) * width] = obuf[i, 0:own, :]

    @pl.when(odd == 1)
    def _():
        for i in range(QUARTERS):
            for b in range(0, width, 256):
                rows = obuf[i, :, b:b + 256].astype(F32)
                mixed[:, i * width + b:i * width + b + 256] = rows[8:8 + own, :].astype(BF16)

    for j in sorted(range(1, ny), key=lambda j: min(j, ny - j)):
        y_copy(j).wait_recv()
        f_copy(j).start()
    for j in range(ny):
        f_copy(j).wait_recv()
    for q in range(QUARTERS):
        for b in range(blocks):
            at = q * width + b * 128
            grads[:, at:at + 128] = gf[b % nk, b // nk, q, 0:LEVELS, :]

    for s in range(2):
        for q in range(2):
            owner, copy = mixed_copy(s, q)
            _, small = loss_copy(s, q)

            @pl.when(owner != z)
            def _():
                copy.wait_send()
                small.wait_send()

    k_copy.wait_send()
    pltpu.make_async_copy(rb, rb, xy_sem.at[0]).wait()
    pltpu.make_async_copy(landed, landed, z_sem.at[0]).wait()
    for j in range(1, ny):
        y_copy(j).wait_send()
    for j in range(ny):
        f_copy(j).wait_send()


def hand_over(mixed, grads, row_loss, mixed_out, grads_out, loss_out, sem):
    copies = [
        pltpu.make_async_copy(src, dst, sem.at[i])
        for i, (src, dst) in enumerate(((mixed, mixed_out), (grads, grads_out), (row_loss, loss_out)))
    ]
    for copy in copies:
        copy.start()
    for copy in copies:
        copy.wait()


def solution(mesh):
    groups = mesh.shape["dp"]
    nk = 2
    ny = 8 if groups == 64 else groups // nk
    nx = groups // (nk * ny)

    def shards(features, segment, gains):
        rows, width = features.shape
        own = rows // RING
        sizes = (groups, nx, ny, nk, own, width, rows * groups)
        half = 2 * own
        lanes = -(-rows // 128) * 128
        vmem = pl.BlockSpec(memory_space=pltpu.VMEM)
        hbm = pl.BlockSpec(memory_space=pltpu.HBM)
        dma = pltpu.SemaphoreType.DMA
        chunks = 2 * half // CHUNK
        mixed, grads, row_loss = pl.pallas_call(
            functools.partial(kernel, sizes),
            out_shape=(
                jax.ShapeDtypeStruct((own, QUARTERS * width), BF16),
                jax.ShapeDtypeStruct((LEVELS, QUARTERS * width), F32),
                jax.ShapeDtypeStruct((1, own), F32),
            ),
            in_specs=[hbm, hbm, hbm],
            out_specs=(vmem, vmem, vmem),
            scratch_shapes=[
                pltpu.VMEM((rows, width), BF16),
                pltpu.VMEM((LEVELS, 2 * half, width), BF16),
                pltpu.VMEM((LEVELS, width), F32),
                pltpu.VMEM((1, own), jnp.int32),
                pltpu.VMEM((2 * half, width), BF16),
                pltpu.VMEM((QUARTERS, 48, width), BF16),
                pltpu.VMEM((RING + 5, 1, lanes + 128), F32),
                pltpu.VMEM((2, 16, 128), BF16),
                pltpu.VMEM((16, 128), F32),
                pltpu.VMEM((HALVES, 16, 128), BF16),
                pltpu.VMEM((2, 16, 128), F32),
                pltpu.VMEM((16, 128), F32),
                pltpu.VMEM((lanes, 128), F32),
                pltpu.VMEM((16, 128), F32),
                pltpu.VMEM((128, lanes), F32),
                pltpu.VMEM((lanes, 128), F32),
                pltpu.VMEM((rows, 128), F32),
                pltpu.VMEM((LEVELS, 8, width), F32),
                pltpu.VMEM((2, 128, 128), F32),
                pltpu.VMEM((2, 1, 128), F32),
                pltpu.VMEM((QUARTERS, 1, 128), F32),
                pltpu.VMEM((nk, ny, 4, 128), F32),
                pltpu.VMEM((ny, 4, 128), F32),
                pltpu.VMEM((ny, 4, 128), F32),
                pltpu.VMEM((nx * ny - 1, 4, 128), F32),
                pltpu.VMEM((RING, 4, 128), F32),
                pltpu.VMEM((nk, ny, QUARTERS, 4, 128), F32),
                dma((HALVES + 4,)),
                dma((2, chunks)), dma((2, chunks)),
                dma((RING - 1,)), dma((RING - 1,)),
                dma((4,)), dma((5,)),
                dma((HALVES,)), dma((2,)),
                dma((4,)), dma((QUARTERS,)),
                dma((4,)), dma((QUARTERS,)),
                dma((2,)), dma((2,)), dma((2,)), dma((ny,)), dma((ny,)), dma((ny,)), dma((ny,)),
            ],
            compiler_params=pltpu.CompilerParams(
                collective_id=0, has_side_effects=True, vmem_limit_bytes=32 * 1024 * 1024),
        )(*(pltpu.with_memory_space_constraint(v, pltpu.HBM) for v in (features, segment.reshape(1, own), gains)))
        mixed, grads, row_loss = pl.pallas_call(
            hand_over,
            out_shape=tuple(jax.ShapeDtypeStruct(v.shape, v.dtype) for v in (mixed, grads, row_loss)),
            in_specs=[vmem] * 3,
            out_specs=(hbm,) * 3,
            scratch_shapes=[dma((3,))],
            compiler_params=pltpu.CompilerParams(vmem_limit_bytes=4 * 1024 * 1024),
        )(mixed, grads, row_loss)
        return mixed, grads, row_loss.reshape(own)

    return jax.shard_map(
        shards,
        mesh=mesh,
        in_specs=(P("dp", "mp"), P(("dp", "mp")), P()),
        out_specs=(P(("dp", "mp"), None), P(), P(("dp", "mp"))),
        check_vma=False,
    )
```

```python
import functools
import math

import jax
import jax.numpy as jnp
from jax import lax
from jax.experimental import pallas as pl
from jax.experimental.pallas import tpu as pltpu
from jax.sharding import PartitionSpec as P

LEVELS = 3
QUARTERS = 4
RING = LEVELS * QUARTERS
HALVES = 6
CHUNK = 16
EPS = 1e-06
F32 = jnp.float32
BF16 = jnp.bfloat16


def first_half(level, quarter):
    return (2 * level + (quarter + 1) // 2 - 1 + HALVES) % HALVES


def handler_level(half, quarter):
    return (((half + HALVES + 1 - (quarter + 1) // 2) % HALVES)) // 2


def kernel(sizes, feat, seg, gains, mixed, grads, row_loss, fbuf, xbuf, gbuf, segbuf, mixbuf, obuf, m1, nr, nrs, nrstage, nrn, nxt,
           sq, segs, scp, cols, val, acc, lq, lrow, lbuf, part, kb, sa, rb, rc, gf,
           local_sem, p1_send, p1_recv, m1_send, m1_recv, mx_send, mx_recv, nr_send, nr_recv, p2_send, p2_recv,
           ls_send, ls_recv, k_sem, xy_sem, z_sem, y_send, y_recv, f_send, f_recv):
    groups, nx, ny, nk, own, width, total_rows = sizes
    half = 2 * own
    group_rows = HALVES * half
    per_half = half // CHUNK
    chunks = 2 * per_half
    blocks = width // 128
    per_piece = blocks // (ny * nk)
    lanes = m1.shape[2] - 128

    g, z = lax.axis_index("dp"), lax.axis_index("mp")
    level, quarter = lax.div(z, QUARTERS), lax.rem(z, QUARTERS)
    a = first_half(level, quarter)
    kc = lax.rem(g, nk)
    y = lax.rem(lax.div(g, nk), ny)
    x = lax.div(g, nk * ny)
    xs = [lax.rem(x + i, nx) * (ny * nk) + kc for i in range(nx)]
    ys = [lax.rem(y + i, ny) for i in range(ny)]
    zs = [lax.rem(z + i, RING) for i in range(RING)]
    plane = [(dx, dy) for dx in range(nx) for dy in range(ny)][1:]
    plane.sort(key=lambda p: -min(p[0], nx - p[0]) - min(p[1], ny - p[1]))
    other = g + 1 - 2 * kc

    def remote(src, dst, send, recv, gd_, zd_):
        return pltpu.make_async_remote_copy(
            src_ref=src, dst_ref=dst, send_sem=send, recv_sem=recv,
            device_id=(gd_, zd_), device_id_type=pl.DeviceIdType.MESH)

    m1[pl.ds(RING, 5), :, 0:lanes] = jnp.zeros((5, 1, lanes), F32)
    m1[pl.ds(RING, 5), :, lanes:lanes + 128] = jnp.full((5, 1, 128), -1.0, F32)
    nr[...] = jnp.zeros(nr.shape, BF16)

    sends_back = jnp.logical_and(jnp.logical_or(z == 0, z >= 2 * QUARTERS), g > 0)
    hears_next = jnp.logical_and(jnp.logical_or(z == 0, z > 2 * QUARTERS), g < groups - 1)
    edge_in = (0, 9, 10, 11)
    edge_out = (8, 9, 10, 11, 0)
    barrier = pltpu.get_barrier_semaphore()

    def greet(gd_, zd_):
        pl.semaphore_signal(barrier, inc=1, device_id=(gd_, zd_), device_id_type=pl.DeviceIdType.MESH)

    for j in (QUARTERS, 2 * QUARTERS, 1, 11, 2, 10, 3, 9, 5, 7, 6):
        greet(g, zs[j])
    @pl.when(sends_back)
    def _():
        for zd in edge_in:
            greet(g - 1, zd)

    @pl.when(hears_next)
    def _():
        for zd in edge_out:
            greet(g + 1, zd)

    greet(other, z)
    for dx, dy in plane:
        greet(xs[dx] + ys[dy] * nk, z)

    loads = []
    for h in range(HALVES):
        loads.append(pltpu.make_async_copy(
            feat.at[pl.ds(h * half, half), :], fbuf.at[pl.ds(h * half, half), :], local_sem.at[h]))
        loads[-1].start()
    gain_load = pltpu.make_async_copy(
        gains.at[:, pl.ds(pl.multiple_of(quarter * width, width), width)], gbuf, local_sem.at[HALVES])
    gain_load.start()
    seg_load = pltpu.make_async_copy(seg, segbuf, local_sem.at[HALVES + 3])
    seg_load.start()
    own_loads = []
    for s in range(2):
        row = pl.multiple_of(((a + s) % HALVES) * half, half)
        own_loads.append(pltpu.make_async_copy(
            feat.at[pl.ds(row, half), :], xbuf.at[level, pl.ds(s * half, half), :], local_sem.at[HALVES + 1 + s]))
        own_loads[-1].start()

    sq[pl.ds(group_rows, sq.shape[0] - group_rows), :] = jnp.zeros((sq.shape[0] - group_rows, 128), F32)
    for h in range(HALVES):
        loads[h].wait()

        def squares(i, _):
            row = pl.multiple_of(h * half + i * CHUNK, CHUNK)
            total = jnp.zeros((CHUNK, 128), F32)
            for b in range(blocks):
                v = fbuf[pl.ds(row, CHUNK), 128 * b:128 * b + 128].astype(F32)
                total = total + v * v
            sq[pl.ds(row, CHUNK), :] = total
            return 0

        lax.fori_loop(0, per_half, squares, 0)
    m1[z, :, 0:lanes] = jnp.sum(sq[...].T, axis=0, keepdims=True)
    seg_load.wait()
    m1[z, :, lanes:lanes + 128] = jnp.zeros((1, 128), F32)
    m1[z, :, lanes:lanes + own] = segbuf[...].astype(F32)

    @pl.when(level == LEVELS - 1)
    def _():
        nrs[...] = jnp.zeros(nrs.shape, F32)
        for h in range(HALVES):
            row = ((h + 1) * half) % group_rows
            for b in range(blocks):
                nrs[b:b + 1, :] = fbuf[row:row + CHUNK, 128 * b:128 * b + 128].astype(F32)[0:1, :]
            nrstage[h] = nrs[...].astype(BF16)

    pl.semaphore_wait(
        barrier, RING - 1 + nk - 1 + len(plane) + jnp.where(sends_back, 4, 0) + jnp.where(hears_next, 5, 0))

    def m1_copy(j):
        return remote(m1.at[z], m1.at[z], m1_send.at[j - 1], m1_recv.at[j - 1], g, zs[j])

    for j in range(1, RING):
        m1_copy(j).start()

    edge_slot = jnp.where(z == 0, 4, quarter)

    def edge_copy(i):
        return remote(m1.at[z], m1.at[RING + edge_slot], mx_send.at[i], mx_recv.at[edge_slot], g - 1, edge_in[i])

    @pl.when(sends_back)
    def _():
        for i in range(4):
            edge_copy(i).start()

    def next_copy(h):
        to = handler_level(h, quarter)
        slot = (h - first_half(to, quarter) + HALVES) % HALVES
        gd_ = g - 1 if h == HALVES - 1 else g
        return remote(nrstage.at[h], nr.at[slot], nr_send.at[h], nr_recv.at[slot], gd_, QUARTERS * to + quarter)

    def next_goes(h):
        if h == HALVES - 1:
            return jnp.logical_and(level == LEVELS - 1, g > 0)
        return jnp.logical_and(level == LEVELS - 1, handler_level(h, quarter) != LEVELS - 1)

    for h in range(HALVES):
        @pl.when(next_goes(h))
        def _():
            next_copy(h).start()

        if h != HALVES - 1:
            @pl.when(jnp.logical_and(level == LEVELS - 1, handler_level(h, quarter) == LEVELS - 1))
            def _():
                slot = (h - first_half(LEVELS - 1, quarter) + HALVES) % HALVES
                nr[slot] = nrstage[h]

    def level_copy(d, k):
        to = (level + d) % LEVELS
        s, kk = k // per_half, k % per_half
        row = ((first_half(to, quarter) + s) % HALVES) * half + kk * CHUNK
        return remote(
            feat.at[pl.ds(pl.multiple_of(row, CHUNK), CHUNK), :],
            xbuf.at[level, pl.ds(pl.multiple_of(k * CHUNK, CHUNK), CHUNK), :],
            p1_send.at[d - 1, k], p1_recv.at[d - 1, k], g, QUARTERS * to + quarter)

    def level_start(i, _):
        k = chunks - 1 - i
        level_copy(1, k).start()
        level_copy(2, k).start()
        return 0

    lax.fori_loop(0, chunks, level_start, 0)

    acc[...] = jnp.zeros(acc.shape, F32)
    lq[...] = jnp.zeros(lq.shape, F32)
    scp[...] = jnp.zeros(scp.shape, F32)
    segs[...] = jnp.zeros(segs.shape, F32)
    gain_load.wait()
    gbuf[...] = gbuf[...] * (1.0 / LEVELS)

    for j in range(1, RING):
        m1_copy(j).wait_recv()

    @pl.when(hears_next)
    def _():
        for i in range(5):
            remote(m1.at[z], m1.at[RING + i], mx_send.at[0], mx_recv.at[i], g, (z + 1) % RING).wait_recv()

    def scale_of(first):
        total = m1[first, :, 0:lanes]
        for i in range(1, QUARTERS):
            total = total + m1[first + i, :, 0:lanes]
        return 1.0 / jnp.sqrt(total * (1.0 / (QUARTERS * width)) + EPS)

    for l in range(LEVELS):
        scp[l:l + 1, :] = scale_of(QUARTERS * l)
    for o in range(RING):
        segs[o:o + 1, :] = m1[o, :, lanes:lanes + 128]
    segs[RING:RING + 1, :] = m1[RING + 4, :, lanes:lanes + 128]
    here = segs[...]
    lane = lax.broadcasted_iota(jnp.int32, here.shape, 1)
    after = jnp.where(lane == own - 1, pltpu.roll(pltpu.roll(here, 15, 0), own - 1, 1), pltpu.roll(here, 127, 1))
    scp[16:32, 0:128] = jnp.where(after == here, 1.0, 0.0)
    cols[...] = scp[...].T
    for o in range(RING):
        val[own * o:own * o + own, :] = jnp.broadcast_to(cols[0:own, 16 + o:17 + o], (own, 128))
    cols[group_rows:group_rows + 8, :] = jnp.broadcast_to(scale_of(RING)[:, 0:1], (8, 128))

    for s in range(2):
        h = (a + s) % HALVES
        comes = jnp.logical_or(jnp.logical_and(h == HALVES - 1, g < groups - 1),
                               jnp.logical_and(h != HALVES - 1, level != LEVELS - 1))

        @pl.when(comes)
        def _():
            remote(nrstage.at[0], nr.at[s], nr_send.at[0], nr_recv.at[s], g, (z + 1) % RING).wait_recv()

        factor = cols[pl.ds(pl.multiple_of((h + 1) * half, 8), 8), :][0:1, LEVELS - 1:LEVELS]
        nrn[s] = nr[s].astype(F32) * factor
    for s in range(2):
        own_loads[s].wait()

    last = lax.broadcasted_iota(jnp.int32, (CHUNK, 128), 0) == CHUNK - 1

    def work(i, _):
        k = chunks - 1 - i
        s, kk = k // per_half, k % per_half
        row = pl.multiple_of(((a + s) % HALVES) * half + kk * CHUNK, CHUNK)
        at = pl.multiple_of(k * CHUNK, CHUNK)
        level_copy(1, k).wait_recv()
        level_copy(2, k).wait_recv()

        @pl.when(kk == per_half - 1)
        def _():
            nxt[...] = nrn[s]

        tile = cols[pl.ds(row, CHUNK), :]
        scales = [jnp.broadcast_to(tile[:, l:l + 1], (CHUNK, 128)) for l in range(LEVELS)]
        ok = val[pl.ds(row, CHUNK), :]
        loss = jnp.zeros((CHUNK, 128), F32)
        for b in range(blocks):
            cs = slice(128 * b, 128 * b + 128)
            unit = [xbuf[l, pl.ds(at, CHUNK), cs].astype(F32) * scales[l] for l in range(LEVELS)]
            joined = unit[0] * gbuf[0:1, cs] + unit[1] * gbuf[1:2, cs] + unit[2] * gbuf[2:3, cs]
            mixbuf[pl.ds(at, CHUNK), cs] = joined.astype(BF16)
            target = jnp.where(last, nxt[b:b + 1, :], pltpu.roll(unit[2], CHUNK - 1, 0))
            nxt[b:b + 1, :] = unit[2][0:1, :]
            error = joined - target
            slope = jnp.clip(error, -1.0, 1.0)
            loss = loss + slope * (error - 0.5 * slope)
            slope = slope * ok
            for l in range(LEVELS):
                term = slope * unit[l]
                acc[l, :, cs] = acc[l, :, cs] + (term[0:8] + term[8:16])
        lq[s, pl.ds(pl.multiple_of(kk * CHUNK, CHUNK), CHUNK), :] = loss * ok
        return 0

    lax.fori_loop(0, chunks, work, 0)

    factor = 1.0 / (math.sqrt(total_rows) * LEVELS)
    part[...] = jnp.zeros(part.shape, F32)
    for b in range(blocks):
        for l in range(LEVELS):
            part[b % nk, b // nk, l:l + 1, :] = factor * jnp.sum(acc[l, :, 128 * b:128 * b + 128], axis=0, keepdims=True)
    k_copy = remote(part.at[1 - kc], kb, k_sem.at[0], k_sem.at[1], other, z)
    k_copy.start()

    for s in range(2):
        lrow[s] = jnp.sum(lq[s].T, axis=0, keepdims=True)

    k_copy.wait_recv()
    sa[...] = part[kc] + kb[...]

    def xy_copy(n):
        dx, dy = plane[n]
        return remote(sa.at[ys[dy]], rb.at[n], xy_sem.at[0], xy_sem.at[1], xs[dx] + ys[dy] * nk, z)

    for n in range(len(plane)):
        xy_copy(n).start()

    for j in range(1, RING):
        m1_copy(j).wait_send()

    @pl.when(sends_back)
    def _():
        for i in range(4):
            edge_copy(i).wait_send()

    for h in range(HALVES):
        @pl.when(next_goes(h))
        def _():
            next_copy(h).wait_send()

    def level_sent(k, _):
        level_copy(1, k).wait_send()
        level_copy(2, k).wait_send()
        return 0

    lax.fori_loop(0, chunks, level_sent, 0)
    pltpu.make_async_copy(rb, rb, xy_sem.at[1]).wait()
    total = sa[y]
    for n in range(len(plane)):
        total = total + rb[n]
    rc[0] = total

    def z_copy(j):
        return remote(rc.at[0], rc.at[j], z_sem.at[0], z_sem.at[1], g, zs[j])

    for j in range(1, RING):
        z_copy(j).start()

    def mixed_copy(s, q):
        owner = 2 * ((a + s) % HALVES) + q
        return owner, remote(mixbuf.at[pl.ds(s * half + 32 * q, 48), :], obuf.at[quarter],
                             p2_send.at[2 * s + q], p2_recv.at[quarter], g, owner)

    def loss_copy(s, q):
        owner = 2 * ((a + s) % HALVES) + q
        return owner, remote(lrow.at[s], lbuf.at[quarter], ls_send.at[2 * s + q], ls_recv.at[quarter], g, owner)

    for s in range(2):
        for q in range(2):
            owner, copy = mixed_copy(s, q)
            _, small = loss_copy(s, q)

            @pl.when(owner != z)
            def _():
                copy.start()
                small.start()

            @pl.when(owner == z)
            def _():
                obuf[quarter] = mixbuf[s * half + 32 * q:s * half + 32 * q + 48, :]
                lbuf[quarter] = lrow[s]

    landed = rc.at[pl.ds(1, RING - 1)]
    pltpu.make_async_copy(landed, landed, z_sem.at[1]).wait()
    for j in range(QUARTERS):
        gf[kc, y, lax.rem(quarter + QUARTERS - j, QUARTERS)] = rc[j] + rc[j + QUARTERS] + rc[j + 2 * QUARTERS]

    def y_copy(j):
        return remote(gf.at[kc, y], gf.at[kc, y], y_send.at[j], y_recv.at[j], xs[0] + ys[j] * nk, z)

    def f_copy(j):
        at = lax.rem(y + ny - j, ny)
        return remote(gf.at[kc, at], gf.at[kc, at], f_send.at[j], f_recv.at[j], other, z)

    for j in range(1, ny):
        y_copy(j).start()
    f_copy(0).start()

    mine, odd = z // 2, z % 2
    for i in range(QUARTERS):
        @pl.when(QUARTERS * handler_level(mine, i) + i != z)
        def _():
            remote(mixbuf.at[pl.ds(0, 48), :], obuf.at[i], p2_send.at[0], p2_recv.at[i], g, (z + 1) % RING).wait_recv()
            remote(lrow.at[0], lbuf.at[i], ls_send.at[0], ls_recv.at[i], g, (z + 1) % RING).wait_recv()

    total = lbuf[0] + lbuf[1] + lbuf[2] + lbuf[3]
    total = total * (1.0 / (QUARTERS * width))
    row_loss[...] = jnp.where(odd == 0, total[:, 0:own], total[:, own:2 * own])

    @pl.when(odd == 0)
    def _():
        for i in range(QUARTERS):
            mixed[:, i * width:(i + 1) * width] = obuf[i, 0:own, :]

    @pl.when(odd == 1)
    def _():
        for i in range(QUARTERS):
            for b in range(0, width, 256):
                rows = obuf[i, :, b:b + 256].astype(F32)
                mixed[:, i * width + b:i * width + b + 256] = rows[8:8 + own, :].astype(BF16)

    for j in sorted(range(1, ny), key=lambda j: min(j, ny - j)):
        y_copy(j).wait_recv()
        f_copy(j).start()
    for j in range(ny):
        f_copy(j).wait_recv()
    for q in range(QUARTERS):
        for b in range(blocks):
            at = q * width + b * 128
            grads[:, at:at + 128] = gf[b % nk, b // nk, q, 0:LEVELS, :]

    for s in range(2):
        for q in range(2):
            owner, copy = mixed_copy(s, q)
            _, small = loss_copy(s, q)

            @pl.when(owner != z)
            def _():
                copy.wait_send()
                small.wait_send()

    k_copy.wait_send()
    pltpu.make_async_copy(rb, rb, xy_sem.at[0]).wait()
    pltpu.make_async_copy(landed, landed, z_sem.at[0]).wait()
    for j in range(1, ny):
        y_copy(j).wait_send()
    for j in range(ny):
        f_copy(j).wait_send()


def hand_over(mixed, grads, row_loss, mixed_out, grads_out, loss_out, sem):
    copies = [
        pltpu.make_async_copy(src, dst, sem.at[i])
        for i, (src, dst) in enumerate(((mixed, mixed_out), (grads, grads_out), (row_loss, loss_out)))
    ]
    for copy in copies:
        copy.start()
    for copy in copies:
        copy.wait()


def solution(mesh):
    groups = mesh.shape["dp"]
    nk = 2
    ny = 8 if groups == 64 else groups // nk
    nx = groups // (nk * ny)

    def shards(features, segment, gains):
        rows, width = features.shape
        own = rows // RING
        sizes = (groups, nx, ny, nk, own, width, rows * groups)
        half = 2 * own
        lanes = -(-rows // 128) * 128
        vmem = pl.BlockSpec(memory_space=pltpu.VMEM)
        hbm = pl.BlockSpec(memory_space=pltpu.HBM)
        dma = pltpu.SemaphoreType.DMA
        chunks = 2 * half // CHUNK
        mixed, grads, row_loss = pl.pallas_call(
            functools.partial(kernel, sizes),
            out_shape=(
                jax.ShapeDtypeStruct((own, QUARTERS * width), BF16),
                jax.ShapeDtypeStruct((LEVELS, QUARTERS * width), F32),
                jax.ShapeDtypeStruct((1, own), F32),
            ),
            in_specs=[hbm, hbm, hbm],
            out_specs=(vmem, vmem, vmem),
            scratch_shapes=[
                pltpu.VMEM((rows, width), BF16),
                pltpu.VMEM((LEVELS, 2 * half, width), BF16),
                pltpu.VMEM((LEVELS, width), F32),
                pltpu.VMEM((1, own), jnp.int32),
                pltpu.VMEM((2 * half, width), BF16),
                pltpu.VMEM((QUARTERS, 48, width), BF16),
                pltpu.VMEM((RING + 5, 1, lanes + 128), F32),
                pltpu.VMEM((2, 16, 128), BF16),
                pltpu.VMEM((16, 128), F32),
                pltpu.VMEM((HALVES, 16, 128), BF16),
                pltpu.VMEM((2, 16, 128), F32),
                pltpu.VMEM((16, 128), F32),
                pltpu.VMEM((lanes, 128), F32),
                pltpu.VMEM((16, 128), F32),
                pltpu.VMEM((128, lanes), F32),
                pltpu.VMEM((lanes, 128), F32),
                pltpu.VMEM((rows, 128), F32),
                pltpu.VMEM((LEVELS, 8, width), F32),
                pltpu.VMEM((2, 128, 128), F32),
                pltpu.VMEM((2, 1, 128), F32),
                pltpu.VMEM((QUARTERS, 1, 128), F32),
                pltpu.VMEM((nk, ny, 4, 128), F32),
                pltpu.VMEM((ny, 4, 128), F32),
                pltpu.VMEM((ny, 4, 128), F32),
                pltpu.VMEM((nx * ny - 1, 4, 128), F32),
                pltpu.VMEM((RING, 4, 128), F32),
                pltpu.VMEM((nk, ny, QUARTERS, 4, 128), F32),
                dma((HALVES + 4,)),
                dma((2, chunks)), dma((2, chunks)),
                dma((RING - 1,)), dma((RING - 1,)),
                dma((4,)), dma((5,)),
                dma((HALVES,)), dma((2,)),
                dma((4,)), dma((QUARTERS,)),
                dma((4,)), dma((QUARTERS,)),
                dma((2,)), dma((2,)), dma((2,)), dma((ny,)), dma((ny,)), dma((ny,)), dma((ny,)),
            ],
            compiler_params=pltpu.CompilerParams(
                collective_id=0, has_side_effects=True, vmem_limit_bytes=32 * 1024 * 1024),
        )(*(pltpu.with_memory_space_constraint(v, pltpu.HBM) for v in (features, segment.reshape(1, own), gains)))
        mixed, grads, row_loss = pl.pallas_call(
            hand_over,
            out_shape=tuple(jax.ShapeDtypeStruct(v.shape, v.dtype) for v in (mixed, grads, row_loss)),
            in_specs=[vmem] * 3,
            out_specs=(hbm,) * 3,
            scratch_shapes=[dma((3,))],
            compiler_params=pltpu.CompilerParams(vmem_limit_bytes=4 * 1024 * 1024),
        )(mixed, grads, row_loss)
        return mixed, grads, row_loss.reshape(own)

    return jax.shard_map(
        shards,
        mesh=mesh,
        in_specs=(P("dp", "mp"), P(("dp", "mp")), P()),
        out_specs=(P(("dp", "mp"), None), P(), P(("dp", "mp"))),
        check_vma=False,
    )
```
